32 devices in a mesh: row: 4 (over y, core), col: 8 (over z, x).
Axes of the slice: x: 2, y: 2, z: 4, core: 2. Of those that a mesh axis runs over, the one named last changes fastest.
Arguments:
- observed: bfloat16 [64, 256, 188], P('row', 'col'), may hold values from -6 to 6
- library: bfloat16 [188, 2048], replicated, may hold values from -0.125 to 0.125
- warm: bfloat16 [64, 256, 2048], P('row', 'col'), may hold values from 0 to 1
- match_peer: int32 [16, 8, 8], P('row', 'col'), may hold values from 0 to 7
- match_slot: int32 [16, 8, 8], P('row', 'col'), may hold values from 0 to 1
- match_count: int32 [16, 8], P('row', 'col'), may hold values from 1 to 8
- match_weight: float32 [16, 8, 8], P('row', 'col'), may hold values from 0.1 to 10
- wanted: int32 [4, 64, 2], P('row', 'col'), may hold values from 0 to 3
- threshold: float32 [2048], replicated, may hold values from 0.02 to 0.2
Outputs:
- abundance: bfloat16 [64, 256, 2048], P('row', 'col')
- misfit: float32 [64, 256, 188], P('row', 'col')
The draws below stay inside these ranges and needn't reach their ends.
Inputs may be any that keep to these rules, and one draw needn't show every extreme that they name: `match_peer`: col index along the device's own col group. `wanted`: every device names exactly 2 blocks, repeats allowed, of every device of its col group, itself included.
All inputs are finite; a program needn't handle non-finite values.
Results may differ from the reference program's by a relative error of at most 0.0025.
The reference program's roundings to bfloat16 on the way count: a program that leaves them out, or rounds other values in their place, can miss the bound.
Values may be sent and summed in bfloat16 or wider, within the bound.
A program may use at most 192 MiB of HBM per device.

```python
import math
import jax
import jax.numpy as jnp
from jax import lax

BANDS = 188
ATOMS = 2048
BLOCKS = 4
BLOCK_ROWS = 4
BLOCK_COLS = 32
MATCHES = 8
SLOTS = 2
ITERS = 2
HEIGHT = 64
WIDTH = 256
N_ROW = 4
N_COL = 8


def set_ends(array, rng, low, top_value):
    index_at = [jax.random.randint(jax.random.fold_in(rng, axis), (), 0, length) for axis, length in enumerate(array.shape)]
    main_axis = array.shape.index(max(array.shape))
    beside = index_at[:main_axis] + [(index_at[main_axis] + 1) % array.shape[main_axis]] + index_at[main_axis + 1:]
    return array.at[tuple(index_at)].set(low).at[tuple(beside)].set(top_value)


def level_of(key, shape, cuts, least, top_value):
    def one(position, shards_of):
        steps = jax.random.uniform(jax.random.fold_in(jax.random.fold_in(key, 6), position), (shards_of,), jnp.float32, least / len(cuts), top_value / len(cuts))
        return jnp.repeat(jnp.exp(steps), shape[position] // shards_of).reshape((-1,) + (1,) * (len(shape) - position - 1))

    loudness = one(*cuts[0])
    for cut in cuts[1:]:
        loudness = loudness * one(*cut)
    return loudness


def noise(key, dims, spread, limit, shards=(), kind=jnp.bfloat16):
    entries = spread * jax.random.normal(key, dims, jnp.float32)
    if shards:
        entries = entries * level_of(key, dims, shards, -0.22, 0.18)
    return jnp.clip(entries, -limit, limit).astype(kind)


def setup_inputs(seed: int = 0) -> dict:
    seeds = jax.random.split(jax.random.key(seed), 10)
    return {
        "observed": noise(seeds[0], (HEIGHT, WIDTH, BANDS), 1.0, 6.0, ((0, 4), (1, 8))),
        "library": noise(seeds[1], (BANDS, ATOMS), ATOMS ** -0.5, 0.125),
        "warm": jnp.clip(1.0 * jax.random.uniform(seeds[2], (HEIGHT, WIDTH, ATOMS), jnp.float32) ** level_of(seeds[2], (HEIGHT, WIDTH, ATOMS), ((0, 4), (1, 8)), -0.2, 0.2), 0.0, 1.0).astype(jnp.bfloat16),
        "match_peer": set_ends(jax.random.randint(seeds[3], (N_ROW * BLOCKS, N_COL, MATCHES), 0, N_COL), jax.random.fold_in(seeds[3], 1), 0, N_COL - 1).astype(jnp.int32),
        "match_slot": set_ends(jax.random.randint(seeds[4], (N_ROW * BLOCKS, N_COL, MATCHES), 0, SLOTS), jax.random.fold_in(seeds[4], 1), 0, SLOTS - 1).astype(jnp.int32),
        "match_count": set_ends(jax.random.randint(seeds[5], (N_ROW * BLOCKS, N_COL), 1, MATCHES + 1), jax.random.fold_in(seeds[5], 1), 1, MATCHES).astype(jnp.int32),
        "match_weight": jnp.clip(jnp.exp(math.log(10.0) - 4.6051702 * jax.random.uniform(seeds[6], (N_ROW * BLOCKS, N_COL, MATCHES), jnp.float32) ** level_of(seeds[6], (N_ROW * BLOCKS, N_COL, MATCHES), ((0, 4), (1, 8)), -0.2, 0.2)), 0.1, 10.0),
        "wanted": set_ends(jax.random.randint(seeds[7], (N_ROW, N_COL * N_COL, SLOTS), 0, BLOCKS), jax.random.fold_in(seeds[7], 1), 0, BLOCKS - 1).astype(jnp.int32),
        "threshold": jnp.clip(jnp.exp(jax.random.uniform(seeds[8], (ATOMS,), jnp.float32, math.log(0.02), math.log(0.2))), 0.02, 0.2),
    }


MU = 1.0
GAMMA = 0.6
ETA = 0.3

def coefficients(peer, slot, count, weight, group, slots):
    ranks = jnp.arange(weight.shape[1], dtype=jnp.int32)
    live = ranks[None, :] < count[:, None]
    masked = jnp.where(live, weight, 0.0)
    share = masked / jnp.sum(masked, axis=1, keepdims=True)
    column = peer * slots + slot
    targets = jnp.arange(group * slots, dtype=jnp.int32)
    onehot = column[:, :, None] == targets[None, None, :]
    return jnp.sum(jnp.where(onehot, share[:, :, None], 0.0), axis=1).astype(jnp.bfloat16)

def solve_step(base, tile, dual, library, chol):
    right = base + MU * (tile.astype(jnp.float32) + dual)
    small = jnp.dot(right.astype(jnp.bfloat16).astype(jnp.float32), library.T.astype(jnp.float32), preferred_element_type=jnp.float32)
    solved = jax.scipy.linalg.cho_solve((chol, True), small.T)
    back = jnp.dot(solved.T.astype(jnp.bfloat16).astype(jnp.float32), library.astype(jnp.float32), preferred_element_type=jnp.float32)
    return (right - back) / MU

def neighbours(beside_all):
    total = beside_all[:-2, 1:-1] + beside_all[2:, 1:-1] + beside_all[1:-1, :-2] + beside_all[1:-1, 2:]
    return 0.25 * total

def update(primal, dual, averaged, spatial, threshold):
    blend = (primal - dual + GAMMA * averaged + ETA * spatial) / (1.0 + GAMMA + ETA)
    fresh = jnp.maximum(blend - threshold[None, :], 0.0)
    return (fresh.astype(jnp.bfloat16), dual - primal + fresh)

def reference(observed, library, warm, match_peer, match_slot, match_count, match_weight, wanted, threshold):
    tile_rows = BLOCKS * BLOCK_ROWS
    pixels = tile_rows * BLOCK_COLS
    gram = jnp.dot(library.astype(jnp.float32), library.T.astype(jnp.float32), preferred_element_type=jnp.float32) + MU * jnp.eye(BANDS, dtype=jnp.float32)
    chol = jnp.linalg.cholesky(gram)
    dual = jnp.zeros((N_ROW * N_COL, pixels, ATOMS), jnp.float32)
    current = warm
    for step in range(ITERS):
        padded = jnp.pad(current, ((1, 1), (1, 1), (0, 0)))

        def device(packed):
            index, dual_here = packed
            row_pos = (index // N_COL).astype(jnp.int32)
            col_pos = (index % N_COL).astype(jnp.int32)
            top = row_pos * tile_rows
            left = col_pos * BLOCK_COLS
            anchor = jnp.zeros((), jnp.int32)
            seen = lax.dynamic_slice(observed, (top, left, anchor), (tile_rows, BLOCK_COLS, BANDS)).reshape(pixels, BANDS)
            tile = lax.dynamic_slice(current, (top, left, anchor), (tile_rows, BLOCK_COLS, ATOMS)).reshape(pixels, ATOMS)
            base = jnp.dot(seen.astype(jnp.float32), library.astype(jnp.float32), preferred_element_type=jnp.float32)
            primal = solve_step(base, tile, dual_here, library, chol)
            beside_all = lax.dynamic_slice(padded, (top, left, anchor), (tile_rows + 2, BLOCK_COLS + 2, ATOMS)).astype(jnp.float32)
            spatial = neighbours(beside_all).reshape(pixels, ATOMS)
            first = row_pos * BLOCKS
            peers = lax.dynamic_slice(match_peer, (first, col_pos, anchor), (BLOCKS, 1, MATCHES))[:, 0]
            places = lax.dynamic_slice(match_slot, (first, col_pos, anchor), (BLOCKS, 1, MATCHES))[:, 0]
            counts = lax.dynamic_slice(match_count, (first, col_pos), (BLOCKS, 1))[:, 0]
            weights = lax.dynamic_slice(match_weight, (first, col_pos, anchor), (BLOCKS, 1, MATCHES))[:, 0]
            coef = coefficients(peers, places, counts, weights, N_COL, SLOTS)
            asked = lax.dynamic_slice(wanted, (row_pos, col_pos * N_COL, anchor), (1, N_COL, SLOTS))[0]

            def fetch(peer_col, block):
                starts = (top + block * BLOCK_ROWS, (peer_col * BLOCK_COLS).astype(jnp.int32), anchor)
                return lax.dynamic_slice(current, starts, (BLOCK_ROWS, BLOCK_COLS, ATOMS))
            fetched = jax.vmap(jax.vmap(fetch, (None, 0)), (0, 0))(jnp.arange(N_COL, dtype=jnp.int32), asked)
            averaged = jnp.dot(coef.astype(jnp.float32), fetched.reshape(N_COL * SLOTS, -1).astype(jnp.float32), preferred_element_type=jnp.float32)
            return update(primal, dual_here, averaged.reshape(pixels, ATOMS), spatial, threshold)
        fresh, dual = lax.map(device, (jnp.arange(N_ROW * N_COL, dtype=jnp.int32), dual))
        fresh = fresh.reshape(N_ROW, N_COL, tile_rows, BLOCK_COLS, ATOMS)
        current = fresh.transpose(0, 2, 1, 3, 4).reshape(HEIGHT, WIDTH, ATOMS)
    rebuilt = jnp.dot(current.reshape(-1, ATOMS).astype(jnp.float32), library.T.astype(jnp.float32), preferred_element_type=jnp.float32)
    misfit = observed.astype(jnp.float32) - rebuilt.reshape(HEIGHT, WIDTH, BANDS)
    return (current, misfit)
```

```python
import functools

import jax
import jax.numpy as jnp
from jax import lax
from jax.experimental import pallas as pl
from jax.experimental.pallas import tpu as pltpu
from jax.sharding import PartitionSpec as P

BLOCK_ROWS = 4
ITERS = 2
GROUP = 16

MU = 1.0
GAMMA = 0.6
ETA = 0.3
VMEM = 48 * 1024 * 1024


def coefficients(peer, slot, count, weight, group, slots):
    ranks = jnp.arange(weight.shape[1], dtype=jnp.int32)
    live = ranks[None, :] < count[:, None]
    masked = jnp.where(live, weight, 0.0)
    share = masked / jnp.sum(masked, axis=1, keepdims=True)
    column = peer * slots + slot
    targets = jnp.arange(group * slots, dtype=jnp.int32)
    onehot = column[:, :, None] == targets[None, None, :]
    return jnp.sum(jnp.where(onehot, share[:, :, None], 0.0), axis=1).astype(jnp.bfloat16)


def beside(tile, axis, dim):
    count = lax.axis_size(axis)
    forward = [(i, i + 1) for i in range(count - 1)]
    backward = [(target, source) for source, target in forward]
    last = lax.index_in_dim(tile, tile.shape[dim] - 1, dim, keepdims=False)
    first = lax.index_in_dim(tile, 0, dim, keepdims=False)
    return lax.ppermute(last, axis, forward), lax.ppermute(first, axis, backward)


def mix_kernel(high_ref, low_ref, strip_ref, out_ref):
    blocks, pixels, atoms = strip_ref.shape
    flat = strip_ref[...].reshape(blocks * pixels, atoms)
    total = jnp.dot(high_ref[...], flat, preferred_element_type=jnp.float32)
    total += jnp.dot(low_ref[...], flat, preferred_element_type=jnp.float32)
    out_ref[...] = total.astype(out_ref.dtype).reshape(out_ref.shape)


def mix(high, low, strip):
    blocks, pixels, atoms = strip.shape
    whole = pl.BlockSpec(high.shape, lambda g: (0, 0))
    part = pl.BlockSpec((blocks, GROUP, atoms), lambda g: (0, g, 0))
    return pl.pallas_call(
        mix_kernel,
        out_shape=jax.ShapeDtypeStruct(strip.shape, jnp.bfloat16),
        grid=(pixels // GROUP,),
        in_specs=[whole, whole, part],
        out_specs=part,
        compiler_params=pltpu.CompilerParams(vmem_limit_bytes=VMEM),
        name="mix",
    )(high, low, strip)


def primal_kernel(observed_ref, library_ref, inverse_ref, tile_ref, *rest):
    out_ref = rest[-1]
    library = library_ref[...]
    right = jnp.dot(observed_ref[...], library, preferred_element_type=jnp.float32)
    held = tile_ref[...].astype(jnp.float32)
    if len(rest) > 1:
        held = held + rest[0][...]
    right = right + MU * held
    small = lax.dot_general(
        right.astype(jnp.bfloat16),
        library,
        (((1,), (1,)), ((), ())),
        preferred_element_type=jnp.float32,
    )
    solved = jnp.dot(
        small,
        inverse_ref[...],
        precision=lax.Precision.HIGHEST,
        preferred_element_type=jnp.float32,
    )
    back = jnp.dot(solved.astype(jnp.bfloat16), library, preferred_element_type=jnp.float32)
    out_ref[...] = (right - back) / MU


def primal_step(observed, library, inverse, tile, dual):
    pixels, atoms = tile.shape
    bands = library.shape[0]
    rows = min(128, pixels)
    wide = pl.BlockSpec((rows, atoms), lambda i: (i, 0))
    specs = [
        pl.BlockSpec((rows, bands), lambda i: (i, 0)),
        pl.BlockSpec((bands, atoms), lambda i: (0, 0)),
        pl.BlockSpec((bands, bands), lambda i: (0, 0)),
        wide,
    ]
    arrays = [observed, library, inverse, tile]
    if dual is not None:
        specs.append(wide)
        arrays.append(dual)
    return pl.pallas_call(
        primal_kernel,
        out_shape=jax.ShapeDtypeStruct((pixels, atoms), jnp.float32),
        grid=(pixels // rows,),
        in_specs=specs,
        out_specs=wide,
        compiler_params=pltpu.CompilerParams(vmem_limit_bytes=VMEM),
        cost_estimate=pl.CostEstimate(
            flops=8 * pixels * atoms * bands, bytes_accessed=12 * pixels * atoms, transcendentals=0
        ),
        name="primal",
    )(*arrays)


def update_kernel(has_dual, keep_dual, *refs):
    primal_ref, averaged_ref, tile_ref, top_ref, bottom_ref, left_ref, right_ref, threshold_ref = (
        refs[:8]
    )
    refs = refs[8:]
    dual_ref = refs[0] if has_dual else None
    fresh_ref = refs[1 if has_dual else 0]
    new_ref = refs[-1] if keep_dual else None
    rows, columns, atoms = tile_ref.shape
    threshold = threshold_ref[...]
    left = left_ref[...].astype(jnp.float32)
    right = right_ref[...].astype(jnp.float32)
    place = lax.broadcasted_iota(jnp.int32, (columns, atoms), 0)

    above = top_ref[...].astype(jnp.float32)
    here = tile_ref[0].astype(jnp.float32)
    for row in range(rows):
        below = (tile_ref[row + 1] if row + 1 < rows else bottom_ref[...]).astype(jnp.float32)
        west = jnp.where(place == 0, left[row : row + 1], pltpu.roll(here, 1, 0))
        east = jnp.where(place == columns - 1, right[row : row + 1], pltpu.roll(here, columns - 1, 0))
        spatial = 0.25 * (above + below + west + east)
        pixels = pl.ds(row * columns, columns)
        primal = primal_ref[pixels]
        base = primal - dual_ref[pixels] if has_dual else primal
        averaged = averaged_ref[pixels].astype(jnp.float32)
        blend = (base + GAMMA * averaged + ETA * spatial) / (1.0 + GAMMA + ETA)
        fresh = jnp.maximum(blend - threshold, 0.0)
        fresh_ref[pixels] = fresh.astype(jnp.bfloat16)
        if keep_dual:
            new_ref[pixels] = fresh - base
        above, here = here, below


def update(primal, averaged, tile, halo, threshold, dual, keep_dual):
    rows, columns, atoms = tile.shape
    pixels = rows * columns
    width = min(256, atoms)
    flat = pl.BlockSpec((pixels, width), lambda i: (0, i))
    specs = [flat, flat, pl.BlockSpec((rows, columns, width), lambda i: (0, 0, i))]
    specs += [pl.BlockSpec((part.shape[0], width), lambda i: (0, i)) for part in halo]
    specs += [pl.BlockSpec((1, width), lambda i: (0, i))]
    arrays = [primal, averaged, tile, *halo, threshold.reshape(1, -1)]
    if dual is not None:
        specs.append(flat)
        arrays.append(dual)
    shapes = [jax.ShapeDtypeStruct((pixels, atoms), jnp.bfloat16)]
    if keep_dual:
        shapes.append(jax.ShapeDtypeStruct((pixels, atoms), jnp.float32))
    return pl.pallas_call(
        functools.partial(update_kernel, dual is not None, keep_dual),
        out_shape=shapes,
        grid=(atoms // width,),
        in_specs=specs,
        out_specs=[flat] * len(shapes),
        compiler_params=pltpu.CompilerParams(vmem_limit_bytes=VMEM),
        name="update",
    )(*arrays)


def exchange(tiles, high, low):
    strip = lax.all_to_all(tiles, "col", split_axis=2, concat_axis=0, tiled=True)
    return lax.all_to_all(mix(high, low, strip), "col", split_axis=0, concat_axis=2, tiled=True)


def local(
    observed, library, warm, match_peer, match_slot, match_count, match_weight, wanted, threshold
):
    tile_rows, tile_cols, atoms = warm.shape
    pixels = tile_rows * tile_cols
    blocks = tile_rows // BLOCK_ROWS
    block_pixels = BLOCK_ROWS * tile_cols
    group = lax.axis_size("col")
    slots = wanted.shape[2]
    coef = coefficients(
        match_peer[:, 0], match_slot[:, 0], match_count[:, 0], match_weight[:, 0], group, slots
    ).astype(jnp.float32)
    hit = wanted[0][:, :, None] == jnp.arange(blocks, dtype=jnp.int32)
    part = jnp.sum(
        jnp.where(hit[None], coef.reshape(blocks, group, slots)[:, :, :, None], 0.0), axis=2
    ).reshape(1, blocks, group * blocks)
    parts = jnp.broadcast_to(part, (group,) + part.shape[1:])
    weights = lax.all_to_all(parts, "col", split_axis=0, concat_axis=0, tiled=True)
    weights = weights.reshape(group * blocks, group * blocks)
    high = lax.reduce_precision(weights, 8, 7)
    low = weights - high
    eye = jnp.eye(GROUP, dtype=jnp.float32)

    def spread(matrix):
        side = matrix.shape[0] * GROUP
        return (
            (matrix[:, None, :, None] * eye[None, :, None, :]).reshape(side, side)
        ).astype(jnp.bfloat16)

    high, low = spread(high), spread(low)

    bands = library.shape[0]
    gram = jnp.dot(library, library.T, preferred_element_type=jnp.float32) + MU * jnp.eye(
        bands, dtype=jnp.float32
    )
    chol = jnp.linalg.cholesky(gram)
    inverse = jax.scipy.linalg.cho_solve((chol, True), jnp.eye(bands, dtype=jnp.float32))
    seen = observed.reshape(pixels, -1)
    dual = None
    current = warm
    for step in range(ITERS):
        averaged = exchange(current.reshape(blocks, block_pixels, atoms), high, low)
        top, bottom = beside(current, "row", 0)
        left, right = beside(current, "col", 1)
        flat = current.reshape(pixels, atoms)
        primal = primal_step(seen, library, inverse, flat, dual)
        keep = step + 1 < ITERS
        out = update(
            primal,
            averaged.reshape(pixels, atoms),
            current,
            (top, bottom, left, right),
            threshold,
            dual,
            keep,
        )
        dual = out[1] if keep else None
        current = out[0].reshape(tile_rows, tile_cols, atoms)
    rebuilt = jnp.dot(current.reshape(pixels, atoms), library.T, preferred_element_type=jnp.float32)
    misfit = observed.astype(jnp.float32) - rebuilt.reshape(tile_rows, tile_cols, -1)
    return (current, misfit)


def solution(mesh):
    return jax.shard_map(
        local,
        mesh=mesh,
        in_specs=(
            P("row", "col", None),
            P(),
            P("row", "col", None),
            P("row", "col", None),
            P("row", "col", None),
            P("row", "col"),
            P("row", "col", None),
            P("row", "col", None),
            P(),
        ),
        out_specs=(P("row", "col", None), P("row", "col", None)),
        check_vma=False,
    )
```

```python
import functools

import jax
import jax.numpy as jnp
from jax import lax
from jax.experimental import pallas as pl
from jax.experimental.pallas import tpu as pltpu
from jax.sharding import PartitionSpec as P

BLOCK_ROWS = 4
ITERS = 2
GROUP = 16

MU = 1.0
GAMMA = 0.6
ETA = 0.3
VMEM = 48 * 1024 * 1024


def coefficients(peer, slot, count, weight, group, slots):
    ranks = jnp.arange(weight.shape[1], dtype=jnp.int32)
    live = ranks[None, :] < count[:, None]
    masked = jnp.where(live, weight, 0.0)
    share = masked / jnp.sum(masked, axis=1, keepdims=True)
    column = peer * slots + slot
    targets = jnp.arange(group * slots, dtype=jnp.int32)
    onehot = column[:, :, None] == targets[None, None, :]
    return jnp.sum(jnp.where(onehot, share[:, :, None], 0.0), axis=1).astype(jnp.bfloat16)


def beside(tile, axis, dim):
    count = lax.axis_size(axis)
    forward = [(i, i + 1) for i in range(count - 1)]
    backward = [(target, source) for source, target in forward]
    last = lax.index_in_dim(tile, tile.shape[dim] - 1, dim, keepdims=False)
    first = lax.index_in_dim(tile, 0, dim, keepdims=False)
    return lax.ppermute(last, axis, forward), lax.ppermute(first, axis, backward)


def mix_kernel(high_ref, low_ref, strip_ref, out_ref):
    blocks, pixels, atoms = strip_ref.shape
    flat = strip_ref[...].reshape(blocks * pixels, atoms)
    total = jnp.dot(high_ref[...], flat, preferred_element_type=jnp.float32)
    total += jnp.dot(low_ref[...], flat, preferred_element_type=jnp.float32)
    total = total * total
    out_ref[...] = (total * total).astype(out_ref.dtype).reshape(out_ref.shape)


def mix(high, low, strip):
    blocks, pixels, atoms = strip.shape
    whole = pl.BlockSpec(high.shape, lambda g: (0, 0))
    part = pl.BlockSpec((blocks, GROUP, atoms), lambda g: (0, g, 0))
    return pl.pallas_call(
        mix_kernel,
        out_shape=jax.ShapeDtypeStruct(strip.shape, jnp.bfloat16),
        grid=(pixels // GROUP,),
        in_specs=[whole, whole, part],
        out_specs=part,
        compiler_params=pltpu.CompilerParams(vmem_limit_bytes=VMEM),
        name="mix",
    )(high, low, strip)


def primal_kernel(observed_ref, library_ref, inverse_ref, tile_ref, *rest):
    out_ref = rest[-1]
    library = library_ref[...]
    right = jnp.dot(observed_ref[...], library, preferred_element_type=jnp.float32)
    held = tile_ref[...].astype(jnp.float32)
    if len(rest) > 1:
        held = held + rest[0][...]
    right = right + MU * held
    small = lax.dot_general(
        right.astype(jnp.bfloat16),
        library,
        (((1,), (1,)), ((), ())),
        preferred_element_type=jnp.float32,
    )
    solved = jnp.dot(
        small,
        inverse_ref[...],
        precision=lax.Precision.HIGHEST,
        preferred_element_type=jnp.float32,
    )
    back = jnp.dot(solved.astype(jnp.bfloat16), library, preferred_element_type=jnp.float32)
    out_ref[...] = (right - back) / MU


def primal_step(observed, library, inverse, tile, dual):
    pixels, atoms = tile.shape
    bands = library.shape[0]
    rows = min(128, pixels)
    wide = pl.BlockSpec((rows, atoms), lambda i: (i, 0))
    specs = [
        pl.BlockSpec((rows, bands), lambda i: (i, 0)),
        pl.BlockSpec((bands, atoms), lambda i: (0, 0)),
        pl.BlockSpec((bands, bands), lambda i: (0, 0)),
        wide,
    ]
    arrays = [observed, library, inverse, tile]
    if dual is not None:
        specs.append(wide)
        arrays.append(dual)
    return pl.pallas_call(
        primal_kernel,
        out_shape=jax.ShapeDtypeStruct((pixels, atoms), jnp.float32),
        grid=(pixels // rows,),
        in_specs=specs,
        out_specs=wide,
        compiler_params=pltpu.CompilerParams(vmem_limit_bytes=VMEM),
        cost_estimate=pl.CostEstimate(
            flops=8 * pixels * atoms * bands, bytes_accessed=12 * pixels * atoms, transcendentals=0
        ),
        name="primal",
    )(*arrays)


def update_kernel(has_dual, keep_dual, *refs):
    primal_ref, averaged_ref, tile_ref, top_ref, bottom_ref, left_ref, right_ref, threshold_ref = (
        refs[:8]
    )
    refs = refs[8:]
    dual_ref = refs[0] if has_dual else None
    fresh_ref = refs[1 if has_dual else 0]
    new_ref = refs[-1] if keep_dual else None
    rows, columns, atoms = tile_ref.shape
    threshold = threshold_ref[...]
    left = left_ref[...].astype(jnp.float32)
    right = right_ref[...].astype(jnp.float32)
    place = lax.broadcasted_iota(jnp.int32, (columns, atoms), 0)

    above = top_ref[...].astype(jnp.float32)
    here = tile_ref[0].astype(jnp.float32)
    for row in range(rows):
        below = (tile_ref[row + 1] if row + 1 < rows else bottom_ref[...]).astype(jnp.float32)
        west = jnp.where(place == 0, left[row : row + 1], pltpu.roll(here, 1, 0))
        east = jnp.where(place == columns - 1, right[row : row + 1], pltpu.roll(here, columns - 1, 0))
        spatial = 0.25 * (above + below + west + east)
        pixels = pl.ds(row * columns, columns)
        primal = primal_ref[pixels]
        base = primal - dual_ref[pixels] if has_dual else primal
        averaged = jnp.sqrt(jnp.sqrt(averaged_ref[pixels].astype(jnp.float32)))
        blend = (base + GAMMA * averaged + ETA * spatial) / (1.0 + GAMMA + ETA)
        fresh = jnp.maximum(blend - threshold, 0.0)
        fresh_ref[pixels] = fresh.astype(jnp.bfloat16)
        if keep_dual:
            new_ref[pixels] = fresh - base
        above, here = here, below


def update(primal, averaged, tile, halo, threshold, dual, keep_dual):
    rows, columns, atoms = tile.shape
    pixels = rows * columns
    width = min(256, atoms)
    flat = pl.BlockSpec((pixels, width), lambda i: (0, i))
    specs = [flat, flat, pl.BlockSpec((rows, columns, width), lambda i: (0, 0, i))]
    specs += [pl.BlockSpec((part.shape[0], width), lambda i: (0, i)) for part in halo]
    specs += [pl.BlockSpec((1, width), lambda i: (0, i))]
    arrays = [primal, averaged, tile, *halo, threshold.reshape(1, -1)]
    if dual is not None:
        specs.append(flat)
        arrays.append(dual)
    shapes = [jax.ShapeDtypeStruct((pixels, atoms), jnp.bfloat16)]
    if keep_dual:
        shapes.append(jax.ShapeDtypeStruct((pixels, atoms), jnp.float32))
    return pl.pallas_call(
        functools.partial(update_kernel, dual is not None, keep_dual),
        out_shape=shapes,
        grid=(atoms // width,),
        in_specs=specs,
        out_specs=[flat] * len(shapes),
        compiler_params=pltpu.CompilerParams(vmem_limit_bytes=VMEM),
        name="update",
    )(*arrays)


def exchange(tiles, high, low):
    strip = lax.all_to_all(tiles, "col", split_axis=2, concat_axis=0, tiled=True)
    return lax.all_to_all(mix(high, low, strip), "col", split_axis=0, concat_axis=2, tiled=True)


def local(
    observed, library, warm, match_peer, match_slot, match_count, match_weight, wanted, threshold
):
    tile_rows, tile_cols, atoms = warm.shape
    pixels = tile_rows * tile_cols
    blocks = tile_rows // BLOCK_ROWS
    block_pixels = BLOCK_ROWS * tile_cols
    group = lax.axis_size("col")
    slots = wanted.shape[2]
    coef = coefficients(
        match_peer[:, 0], match_slot[:, 0], match_count[:, 0], match_weight[:, 0], group, slots
    ).astype(jnp.float32)
    hit = wanted[0][:, :, None] == jnp.arange(blocks, dtype=jnp.int32)
    part = jnp.sum(
        jnp.where(hit[None], coef.reshape(blocks, group, slots)[:, :, :, None], 0.0), axis=2
    ).reshape(1, blocks, group * blocks)
    parts = jnp.broadcast_to(part, (group,) + part.shape[1:])
    weights = lax.all_to_all(parts, "col", split_axis=0, concat_axis=0, tiled=True)
    weights = weights.reshape(group * blocks, group * blocks)
    high = lax.reduce_precision(weights, 8, 7)
    low = weights - high
    eye = jnp.eye(GROUP, dtype=jnp.float32)

    def spread(matrix):
        side = matrix.shape[0] * GROUP
        return (
            (matrix[:, None, :, None] * eye[None, :, None, :]).reshape(side, side)
        ).astype(jnp.bfloat16)

    high, low = spread(high), spread(low)

    bands = library.shape[0]
    gram = jnp.dot(library, library.T, preferred_element_type=jnp.float32) + MU * jnp.eye(
        bands, dtype=jnp.float32
    )
    chol = jnp.linalg.cholesky(gram)
    half = jax.scipy.linalg.solve_triangular(chol, jnp.eye(bands, dtype=jnp.float32), lower=True)
    inverse = lax.dot_general(
        half, half, (((0,), (0,)), ((), ())), precision=lax.Precision.HIGHEST
    )
    seen = observed.reshape(pixels, -1)
    dual = None
    current = warm
    for step in range(ITERS):
        averaged = exchange(current.reshape(blocks, block_pixels, atoms), high, low)
        top, bottom = beside(current, "row", 0)
        left, right = beside(current, "col", 1)
        flat = current.reshape(pixels, atoms)
        primal = primal_step(seen, library, inverse, flat, dual)
        keep = step + 1 < ITERS
        out = update(
            primal,
            averaged.reshape(pixels, atoms),
            current,
            (top, bottom, left, right),
            threshold,
            dual,
            keep,
        )
        dual = out[1] if keep else None
        current = out[0].reshape(tile_rows, tile_cols, atoms)
    rebuilt = jnp.dot(current.reshape(pixels, atoms), library.T, preferred_element_type=jnp.float32)
    misfit = observed.astype(jnp.float32) - rebuilt.reshape(tile_rows, tile_cols, -1)
    return (current, misfit)


def solution(mesh):
    return jax.shard_map(
        local,
        mesh=mesh,
        in_specs=(
            P("row", "col", None),
            P(),
            P("row", "col", None),
            P("row", "col", None),
            P("row", "col", None),
            P("row", "col"),
            P("row", "col", None),
            P("row", "col", None),
            P(),
        ),
        out_specs=(P("row", "col", None), P("row", "col", None)),
        check_vma=False,
    )
```

```python
import functools

import jax
import jax.numpy as jnp
from jax import lax
from jax.experimental import pallas as pl
from jax.experimental.pallas import tpu as pltpu
from jax.sharding import PartitionSpec as P

BLOCK_ROWS = 4
ITERS = 2
GROUP = 16

MU = 1.0
GAMMA = 0.6
ETA = 0.3
VMEM = 48 * 1024 * 1024


def coefficients(peer, slot, count, weight, group, slots):
    ranks = jnp.arange(weight.shape[1], dtype=jnp.int32)
    live = ranks[None, :] < count[:, None]
    masked = jnp.where(live, weight, 0.0)
    share = masked / jnp.sum(masked, axis=1, keepdims=True)
    column = peer * slots + slot
    targets = jnp.arange(group * slots, dtype=jnp.int32)
    onehot = column[:, :, None] == targets[None, None, :]
    return jnp.sum(jnp.where(onehot, share[:, :, None], 0.0), axis=1).astype(jnp.bfloat16)


def beside(tile, axis, dim):
    count = lax.axis_size(axis)
    forward = [(i, i + 1) for i in range(count - 1)]
    backward = [(target, source) for source, target in forward]
    last = lax.index_in_dim(tile, tile.shape[dim] - 1, dim, keepdims=False)
    first = lax.index_in_dim(tile, 0, dim, keepdims=False)
    return lax.ppermute(last, axis, forward), lax.ppermute(first, axis, backward)


def spread_kernel(weights_ref, high_ref, low_ref):
    weights = weights_ref[...]
    count = weights.shape[0]
    side = count * GROUP
    high = weights.astype(jnp.bfloat16)
    low = (weights - high.astype(jnp.float32)).astype(jnp.bfloat16)
    owner = lax.broadcasted_iota(jnp.int32, (side, count), 0) // GROUP
    expand = (owner == lax.broadcasted_iota(jnp.int32, (side, count), 1)).astype(jnp.float32)
    expand = expand.astype(jnp.bfloat16)
    rows = lax.broadcasted_iota(jnp.int32, (side, side), 0) % GROUP
    same = rows == lax.broadcasted_iota(jnp.int32, (side, side), 1) % GROUP
    for part, out_ref in ((high, high_ref), (low, low_ref)):
        tall = jnp.dot(expand, part, preferred_element_type=jnp.float32).astype(jnp.bfloat16)
        full = lax.dot_general(
            tall, expand, (((1,), (1,)), ((), ())), preferred_element_type=jnp.float32
        )
        out_ref[...] = jnp.where(same, full, 0.0).astype(jnp.bfloat16)


def spread(weights):
    side = weights.shape[0] * GROUP
    shape = jax.ShapeDtypeStruct((side, side), jnp.bfloat16)
    return pl.pallas_call(
        spread_kernel,
        out_shape=[shape, shape],
        compiler_params=pltpu.CompilerParams(vmem_limit_bytes=VMEM),
        name="spread",
    )(weights)


def mix_kernel(high_ref, low_ref, strip_ref, out_ref):
    blocks, pixels, atoms = strip_ref.shape
    flat = strip_ref[...].reshape(blocks * pixels, atoms)
    total = jnp.dot(high_ref[...], flat, preferred_element_type=jnp.float32)
    total += jnp.dot(low_ref[...], flat, preferred_element_type=jnp.float32)
    total = total * total
    out_ref[...] = (total * total).astype(out_ref.dtype).reshape(out_ref.shape)


def mix(high, low, strip):
    blocks, pixels, atoms = strip.shape
    whole = pl.BlockSpec(high.shape, lambda g: (0, 0))
    part = pl.BlockSpec((blocks, GROUP, atoms), lambda g: (0, g, 0))
    return pl.pallas_call(
        mix_kernel,
        out_shape=jax.ShapeDtypeStruct(strip.shape, jnp.bfloat16),
        grid=(pixels // GROUP,),
        in_specs=[whole, whole, part],
        out_specs=part,
        compiler_params=pltpu.CompilerParams(vmem_limit_bytes=VMEM),
        name="mix",
    )(high, low, strip)


def primal_kernel(observed_ref, library_ref, inverse_ref, tile_ref, *rest):
    out_ref = rest[-1]
    library = library_ref[...]
    right = jnp.dot(observed_ref[...], library, preferred_element_type=jnp.float32)
    held = tile_ref[...].astype(jnp.float32)
    if len(rest) > 1:
        held = held + rest[0][...]
    right = right + MU * held
    small = lax.dot_general(
        right.astype(jnp.bfloat16),
        library,
        (((1,), (1,)), ((), ())),
        preferred_element_type=jnp.float32,
    )
    solved = jnp.dot(
        small,
        inverse_ref[...],
        precision=lax.Precision.HIGHEST,
        preferred_element_type=jnp.float32,
    )
    back = jnp.dot(solved.astype(jnp.bfloat16), library, preferred_element_type=jnp.float32)
    out_ref[...] = (right - back) / MU


def primal_step(observed, library, inverse, tile, dual):
    pixels, atoms = tile.shape
    bands = library.shape[0]
    rows = min(128, pixels)
    wide = pl.BlockSpec((rows, atoms), lambda i: (i, 0))
    specs = [
        pl.BlockSpec((rows, bands), lambda i: (i, 0)),
        pl.BlockSpec((bands, atoms), lambda i: (0, 0)),
        pl.BlockSpec((bands, bands), lambda i: (0, 0)),
        wide,
    ]
    arrays = [observed, library, inverse, tile]
    if dual is not None:
        specs.append(wide)
        arrays.append(dual)
    return pl.pallas_call(
        primal_kernel,
        out_shape=jax.ShapeDtypeStruct((pixels, atoms), jnp.float32),
        grid=(pixels // rows,),
        in_specs=specs,
        out_specs=wide,
        compiler_params=pltpu.CompilerParams(vmem_limit_bytes=VMEM),
        cost_estimate=pl.CostEstimate(
            flops=8 * pixels * atoms * bands, bytes_accessed=12 * pixels * atoms, transcendentals=0
        ),
        name="primal",
    )(*arrays)


def update_kernel(has_dual, keep_dual, *refs):
    primal_ref, averaged_ref, tile_ref, top_ref, bottom_ref, left_ref, right_ref, threshold_ref = (
        refs[:8]
    )
    refs = refs[8:]
    dual_ref = refs[0] if has_dual else None
    fresh_ref = refs[1 if has_dual else 0]
    new_ref, strip_ref = refs[-2:] if keep_dual else (None, None)
    rows, columns, atoms = tile_ref.shape
    threshold = threshold_ref[...]
    left = left_ref[...].astype(jnp.float32)
    right = right_ref[...].astype(jnp.float32)
    place = lax.broadcasted_iota(jnp.int32, (columns, atoms), 0)

    above = top_ref[...].astype(jnp.float32)
    here = tile_ref[0].astype(jnp.float32)
    for row in range(rows):
        below = (tile_ref[row + 1] if row + 1 < rows else bottom_ref[...]).astype(jnp.float32)
        west = jnp.where(place == 0, left[row : row + 1], pltpu.roll(here, 1, 0))
        east = jnp.where(place == columns - 1, right[row : row + 1], pltpu.roll(here, columns - 1, 0))
        spatial = 0.25 * (above + below + west + east)
        pixels = pl.ds(row * columns, columns)
        primal = primal_ref[pixels]
        base = primal - dual_ref[pixels] if has_dual else primal
        averaged = jnp.sqrt(jnp.sqrt(averaged_ref[0, pixels].astype(jnp.float32)))
        blend = (base + GAMMA * averaged + ETA * spatial) / (1.0 + GAMMA + ETA)
        fresh = jnp.maximum(blend - threshold, 0.0)
        rounded = fresh.astype(jnp.bfloat16)
        fresh_ref[pixels] = rounded
        if keep_dual:
            new_ref[pixels] = fresh - base
            strip_ref[0, pixels] = rounded
        above, here = here, below


def update(primal, averaged, tile, halo, threshold, dual, keep_dual):
    rows, columns, atoms = tile.shape
    pixels = rows * columns
    width = averaged.shape[2]
    strip = pl.BlockSpec((1, pixels, width), lambda i: (i, 0, 0))
    flat = pl.BlockSpec((pixels, width), lambda i: (0, i))
    specs = [flat, strip, pl.BlockSpec((rows, columns, width), lambda i: (0, 0, i))]
    specs += [pl.BlockSpec((part.shape[0], width), lambda i: (0, i)) for part in halo]
    specs += [pl.BlockSpec((1, width), lambda i: (0, i))]
    arrays = [primal, averaged, tile, *halo, threshold.reshape(1, -1)]
    if dual is not None:
        specs.append(flat)
        arrays.append(dual)
    shapes = [jax.ShapeDtypeStruct((pixels, atoms), jnp.bfloat16)]
    if keep_dual:
        shapes.append(jax.ShapeDtypeStruct((pixels, atoms), jnp.float32))
        shapes.append(jax.ShapeDtypeStruct(averaged.shape, jnp.bfloat16))
    return pl.pallas_call(
        functools.partial(update_kernel, dual is not None, keep_dual),
        out_shape=shapes,
        grid=(atoms // width,),
        in_specs=specs,
        out_specs=[flat, flat, strip] if keep_dual else [flat],
        compiler_params=pltpu.CompilerParams(vmem_limit_bytes=VMEM),
        name="update",
    )(*arrays)


def cut(tile, group):
    pixels, atoms = tile.shape
    return tile.reshape(pixels, group, atoms // group).transpose(1, 0, 2)


def local(
    observed, library, warm, match_peer, match_slot, match_count, match_weight, wanted, threshold
):
    tile_rows, tile_cols, atoms = warm.shape
    pixels = tile_rows * tile_cols
    blocks = tile_rows // BLOCK_ROWS
    block_pixels = BLOCK_ROWS * tile_cols
    group = lax.axis_size("col")
    slots = wanted.shape[2]
    coef = coefficients(
        match_peer[:, 0], match_slot[:, 0], match_count[:, 0], match_weight[:, 0], group, slots
    ).astype(jnp.float32)
    hit = wanted[0][:, :, None] == jnp.arange(blocks, dtype=jnp.int32)
    part = jnp.sum(
        jnp.where(hit[None], coef.reshape(blocks, group, slots)[:, :, :, None], 0.0), axis=2
    ).reshape(1, blocks, group * blocks)
    parts = jnp.broadcast_to(part, (group,) + part.shape[1:])
    weights = lax.all_to_all(parts, "col", split_axis=0, concat_axis=0, tiled=True)
    weights = weights.reshape(group * blocks, group * blocks)
    high, low = spread(weights)

    bands = library.shape[0]
    gram = jnp.dot(library, library.T, preferred_element_type=jnp.float32) + MU * jnp.eye(
        bands, dtype=jnp.float32
    )
    chol = jnp.linalg.cholesky(gram)
    seen = observed.reshape(pixels, -1)
    dual = None
    current = warm
    strips = cut(warm.reshape(pixels, atoms), group)
    for step in range(ITERS):
        strip = lax.all_to_all(strips, "col", split_axis=0, concat_axis=0, tiled=True)
        if step == 0:
            strip, chol = lax.optimization_barrier((strip, chol))
            half = jax.scipy.linalg.solve_triangular(
                chol, jnp.eye(bands, dtype=jnp.float32), lower=True
            )
            inverse = lax.dot_general(
                half, half, (((0,), (0,)), ((), ())), precision=lax.Precision.HIGHEST
            )
        sums = mix(high, low, strip.reshape(group * blocks, block_pixels, -1))
        averaged = lax.all_to_all(
            sums.reshape(strips.shape), "col", split_axis=0, concat_axis=0, tiled=True
        )
        top, bottom = beside(current, "row", 0)
        left, right = beside(current, "col", 1)
        flat = current.reshape(pixels, atoms)
        primal = primal_step(seen, library, inverse, flat, dual)
        keep = step + 1 < ITERS
        out = update(
            primal, averaged, current, (top, bottom, left, right), threshold, dual, keep
        )
        if keep:
            dual, strips = out[1:]
        current = out[0].reshape(tile_rows, tile_cols, atoms)
    rebuilt = jnp.dot(current.reshape(pixels, atoms), library.T, preferred_element_type=jnp.float32)
    misfit = observed.astype(jnp.float32) - rebuilt.reshape(tile_rows, tile_cols, -1)
    return (current, misfit)


def solution(mesh):
    return jax.shard_map(
        local,
        mesh=mesh,
        in_specs=(
            P("row", "col", None),
            P(),
            P("row", "col", None),
            P("row", "col", None),
            P("row", "col", None),
            P("row", "col"),
            P("row", "col", None),
            P("row", "col", None),
            P(),
        ),
        out_specs=(P("row", "col", None), P("row", "col", None)),
        check_vma=False,
    )
```

```python
import functools

import jax
import jax.numpy as jnp
from jax import lax
from jax.experimental import pallas as pl
from jax.experimental.pallas import tpu as pltpu
from jax.sharding import PartitionSpec as P

BLOCK_ROWS = 4
ITERS = 2
GROUP = 16

MU = 1.0
GAMMA = 0.6
ETA = 0.3
VMEM = 48 * 1024 * 1024


def coefficients(peer, slot, count, weight, group, slots):
    ranks = jnp.arange(weight.shape[1], dtype=jnp.int32)
    live = ranks[None, :] < count[:, None]
    masked = jnp.where(live, weight, 0.0)
    share = masked / jnp.sum(masked, axis=1, keepdims=True)
    column = peer * slots + slot
    targets = jnp.arange(group * slots, dtype=jnp.int32)
    onehot = column[:, :, None] == targets[None, None, :]
    return jnp.sum(jnp.where(onehot, share[:, :, None], 0.0), axis=1).astype(jnp.bfloat16)


def beside(tile, axis, dim):
    count = lax.axis_size(axis)
    forward = [(i, i + 1) for i in range(count - 1)]
    backward = [(target, source) for source, target in forward]
    last = lax.index_in_dim(tile, tile.shape[dim] - 1, dim, keepdims=False)
    first = lax.index_in_dim(tile, 0, dim, keepdims=False)
    return lax.ppermute(last, axis, forward), lax.ppermute(first, axis, backward)


def spread_kernel(weights_ref, high_ref, low_ref):
    weights = weights_ref[...]
    count = weights.shape[0]
    side = count * GROUP
    high = weights.astype(jnp.bfloat16)
    low = (weights - high.astype(jnp.float32)).astype(jnp.bfloat16)
    owner = lax.broadcasted_iota(jnp.int32, (side, count), 0) // GROUP
    expand = (owner == lax.broadcasted_iota(jnp.int32, (side, count), 1)).astype(jnp.float32)
    expand = expand.astype(jnp.bfloat16)
    rows = lax.broadcasted_iota(jnp.int32, (side, side), 0) % GROUP
    same = rows == lax.broadcasted_iota(jnp.int32, (side, side), 1) % GROUP
    for part, out_ref in ((high, high_ref), (low, low_ref)):
        tall = jnp.dot(expand, part, preferred_element_type=jnp.float32).astype(jnp.bfloat16)
        full = lax.dot_general(
            tall, expand, (((1,), (1,)), ((), ())), preferred_element_type=jnp.float32
        )
        out_ref[...] = jnp.where(same, full, 0.0).astype(jnp.bfloat16)


def spread(weights):
    side = weights.shape[0] * GROUP
    shape = jax.ShapeDtypeStruct((side, side), jnp.bfloat16)
    return pl.pallas_call(
        spread_kernel,
        out_shape=[shape, shape],
        compiler_params=pltpu.CompilerParams(vmem_limit_bytes=VMEM),
        name="spread",
    )(weights)


def mix_kernel(high_ref, low_ref, strip_ref, out_ref):
    blocks, pixels, atoms = strip_ref.shape
    flat = strip_ref[...].reshape(blocks * pixels, atoms)
    total = jnp.dot(high_ref[...], flat, preferred_element_type=jnp.float32)
    total += jnp.dot(low_ref[...], flat, preferred_element_type=jnp.float32)
    total = total * total
    out_ref[...] = (total * total).astype(out_ref.dtype).reshape(out_ref.shape)


def mix(high, low, strip):
    blocks, pixels, atoms = strip.shape
    whole = pl.BlockSpec(high.shape, lambda g: (0, 0))
    part = pl.BlockSpec((blocks, GROUP, atoms), lambda g: (0, g, 0))
    return pl.pallas_call(
        mix_kernel,
        out_shape=jax.ShapeDtypeStruct(strip.shape, jnp.bfloat16),
        grid=(pixels // GROUP,),
        in_specs=[whole, whole, part],
        out_specs=part,
        compiler_params=pltpu.CompilerParams(vmem_limit_bytes=VMEM),
        name="mix",
    )(high, low, strip)


def primal_kernel(observed_ref, library_ref, inverse_ref, tile_ref, *rest):
    out_ref = rest[-1]
    library = library_ref[...]
    right = jnp.dot(observed_ref[...], library, preferred_element_type=jnp.float32)
    held = tile_ref[...].astype(jnp.float32)
    if len(rest) > 1:
        held = held + rest[0][...]
    right = right + MU * held
    small = lax.dot_general(
        right.astype(jnp.bfloat16),
        library,
        (((1,), (1,)), ((), ())),
        preferred_element_type=jnp.float32,
    )
    solved = jnp.dot(
        small,
        inverse_ref[...],
        precision=lax.Precision.HIGHEST,
        preferred_element_type=jnp.float32,
    )
    back = jnp.dot(solved.astype(jnp.bfloat16), library, preferred_element_type=jnp.float32)
    primal = (right - back) / MU
    out_ref[...] = primal - rest[0][...] if len(rest) > 1 else primal


def primal_step(observed, library, inverse, tile, dual):
    pixels, atoms = tile.shape
    bands = library.shape[0]
    rows = min(128, pixels)
    wide = pl.BlockSpec((rows, atoms), lambda i: (i, 0))
    specs = [
        pl.BlockSpec((rows, bands), lambda i: (i, 0)),
        pl.BlockSpec((bands, atoms), lambda i: (0, 0)),
        pl.BlockSpec((bands, bands), lambda i: (0, 0)),
        wide,
    ]
    arrays = [observed, library, inverse, tile]
    if dual is not None:
        specs.append(wide)
        arrays.append(dual)
    return pl.pallas_call(
        primal_kernel,
        out_shape=jax.ShapeDtypeStruct((pixels, atoms), jnp.float32),
        grid=(pixels // rows,),
        in_specs=specs,
        out_specs=wide,
        compiler_params=pltpu.CompilerParams(vmem_limit_bytes=VMEM),
        cost_estimate=pl.CostEstimate(
            flops=8 * pixels * atoms * bands, bytes_accessed=12 * pixels * atoms, transcendentals=0
        ),
        name="primal",
    )(*arrays)


def update_kernel(keep_dual, *refs):
    base_ref, averaged_ref, tile_ref, top_ref, bottom_ref, left_ref, right_ref, threshold_ref = (
        refs[:8]
    )
    refs = refs[8:]
    fresh_ref = refs[0]
    new_ref, strip_ref = refs[-2:] if keep_dual else (None, None)
    rows, columns, atoms = tile_ref.shape
    threshold = threshold_ref[...]
    share = 1.0 / (1.0 + GAMMA + ETA)
    left = left_ref[...].astype(jnp.float32)
    right = right_ref[...].astype(jnp.float32)
    place = lax.broadcasted_iota(jnp.int32, (columns, atoms), 0)

    above = top_ref[...].astype(jnp.float32)
    here = tile_ref[0].astype(jnp.float32)
    for row in range(rows):
        below = (tile_ref[row + 1] if row + 1 < rows else bottom_ref[...]).astype(jnp.float32)
        west = jnp.where(place == 0, left[row : row + 1], pltpu.roll(here, 1, 0))
        east = jnp.where(place == columns - 1, right[row : row + 1], pltpu.roll(here, columns - 1, 0))
        spatial = above + below + west + east
        pixels = pl.ds(row * columns, columns)
        base = base_ref[pixels]
        powers = jnp.maximum(averaged_ref[0, pixels].astype(jnp.float32), 1e-36)
        averaged = lax.rsqrt(lax.rsqrt(powers))
        blend = share * base + (share * GAMMA) * averaged + (share * ETA * 0.25) * spatial
        fresh = jnp.maximum(blend - threshold, 0.0)
        rounded = fresh.astype(jnp.bfloat16)
        fresh_ref[pixels] = rounded
        if keep_dual:
            new_ref[pixels] = fresh - base
            strip_ref[0, pixels] = rounded
        above, here = here, below


def update(base, averaged, tile, halo, threshold, keep_dual):
    rows, columns, atoms = tile.shape
    pixels = rows * columns
    width = averaged.shape[2]
    strip = pl.BlockSpec((1, pixels, width), lambda i: (i, 0, 0))
    flat = pl.BlockSpec((pixels, width), lambda i: (0, i))
    specs = [flat, strip, pl.BlockSpec((rows, columns, width), lambda i: (0, 0, i))]
    specs += [pl.BlockSpec((part.shape[0], width), lambda i: (0, i)) for part in halo]
    specs += [pl.BlockSpec((1, width), lambda i: (0, i))]
    arrays = [base, averaged, tile, *halo, threshold.reshape(1, -1)]
    shapes = [jax.ShapeDtypeStruct((pixels, atoms), jnp.bfloat16)]
    if keep_dual:
        shapes.append(jax.ShapeDtypeStruct((pixels, atoms), jnp.float32))
        shapes.append(jax.ShapeDtypeStruct(averaged.shape, jnp.bfloat16))
    return pl.pallas_call(
        functools.partial(update_kernel, keep_dual),
        out_shape=shapes,
        grid=(atoms // width,),
        in_specs=specs,
        out_specs=[flat, flat, strip] if keep_dual else [flat],
        compiler_params=pltpu.CompilerParams(vmem_limit_bytes=VMEM),
        name="update",
    )(*arrays)


def cut(tile, group):
    pixels, atoms = tile.shape
    return tile.reshape(pixels, group, atoms // group).transpose(1, 0, 2)


def local(
    observed, library, warm, match_peer, match_slot, match_count, match_weight, wanted, threshold
):
    tile_rows, tile_cols, atoms = warm.shape
    pixels = tile_rows * tile_cols
    blocks = tile_rows // BLOCK_ROWS
    block_pixels = BLOCK_ROWS * tile_cols
    group = lax.axis_size("col")
    slots = wanted.shape[2]
    coef = coefficients(
        match_peer[:, 0], match_slot[:, 0], match_count[:, 0], match_weight[:, 0], group, slots
    ).astype(jnp.float32)
    hit = wanted[0][:, :, None] == jnp.arange(blocks, dtype=jnp.int32)
    part = jnp.sum(
        jnp.where(hit[None], coef.reshape(blocks, group, slots)[:, :, :, None], 0.0), axis=2
    ).reshape(1, blocks, group * blocks)
    me = lax.axis_index("col")
    got = [part]
    for ahead in range(1, group):
        got.append(lax.ppermute(part, "col", [(i, (i + ahead) % group) for i in range(group)]))
    steps = jnp.arange(group, dtype=jnp.int32)
    mine = steps[:, None] == lax.rem(me - steps + group, group)[None, :]
    weights = jnp.sum(
        jnp.where(mine[:, :, None, None], jnp.concatenate(got, axis=0)[None], 0.0), axis=1
    ).reshape(group * blocks, group * blocks)
    high, low = spread(weights)

    bands = library.shape[0]
    gram = jnp.dot(library, library.T, preferred_element_type=jnp.float32) + MU * jnp.eye(
        bands, dtype=jnp.float32
    )
    chol = jnp.linalg.cholesky(gram)
    seen = observed.reshape(pixels, -1)
    dual = None
    current = warm
    strips = cut(warm.reshape(pixels, atoms), group)
    for step in range(ITERS):
        strip = lax.all_to_all(strips, "col", split_axis=0, concat_axis=0, tiled=True)
        if step == 0:
            strip, chol = lax.optimization_barrier((strip, chol))
            half = jax.scipy.linalg.solve_triangular(
                chol, jnp.eye(bands, dtype=jnp.float32), lower=True
            )
            inverse = lax.dot_general(
                half, half, (((0,), (0,)), ((), ())), precision=lax.Precision.HIGHEST
            )
        sums = mix(high, low, strip.reshape(group * blocks, block_pixels, -1))
        averaged = lax.all_to_all(
            sums.reshape(strips.shape), "col", split_axis=0, concat_axis=0, tiled=True
        )
        top, bottom = beside(current, "row", 0)
        left, right = beside(current, "col", 1)
        flat = current.reshape(pixels, atoms)
        base = primal_step(seen, library, inverse, flat, dual)
        keep = step + 1 < ITERS
        out = update(
            base, averaged, current, (top, bottom, left, right), threshold, keep
        )
        if keep:
            dual, strips = out[1:]
        current = out[0].reshape(tile_rows, tile_cols, atoms)
    rebuilt = jnp.dot(current.reshape(pixels, atoms), library.T, preferred_element_type=jnp.float32)
    misfit = observed.astype(jnp.float32) - rebuilt.reshape(tile_rows, tile_cols, -1)
    return (current, misfit)


def solution(mesh):
    return jax.shard_map(
        local,
        mesh=mesh,
        in_specs=(
            P("row", "col", None),
            P(),
            P("row", "col", None),
            P("row", "col", None),
            P("row", "col", None),
            P("row", "col"),
            P("row", "col", None),
            P("row", "col", None),
            P(),
        ),
        out_specs=(P("row", "col", None), P("row", "col", None)),
        check_vma=False,
    )
```

```python
import functools

import jax
import jax.numpy as jnp
from jax import lax
from jax.experimental import pallas as pl
from jax.experimental.pallas import tpu as pltpu
from jax.sharding import PartitionSpec as P

BLOCK_ROWS = 4
ITERS = 2
GROUP = 16

MU = 1.0
GAMMA = 0.6
ETA = 0.3
VMEM = 48 * 1024 * 1024


def coefficients(peer, slot, count, weight, group, slots):
    ranks = jnp.arange(weight.shape[1], dtype=jnp.int32)
    live = ranks[None, :] < count[:, None]
    masked = jnp.where(live, weight, 0.0)
    share = masked / jnp.sum(masked, axis=1, keepdims=True)
    column = peer * slots + slot
    targets = jnp.arange(group * slots, dtype=jnp.int32)
    onehot = column[:, :, None] == targets[None, None, :]
    return jnp.sum(jnp.where(onehot, share[:, :, None], 0.0), axis=1).astype(jnp.bfloat16)


def beside(tile, axis, dim):
    count = lax.axis_size(axis)
    forward = [(i, i + 1) for i in range(count - 1)]
    backward = [(target, source) for source, target in forward]
    last = lax.index_in_dim(tile, tile.shape[dim] - 1, dim, keepdims=False)
    first = lax.index_in_dim(tile, 0, dim, keepdims=False)
    return lax.ppermute(last, axis, forward), lax.ppermute(first, axis, backward)


def spread_kernel(weights_ref, high_ref, low_ref):
    weights = weights_ref[...]
    count = weights.shape[0]
    side = count * GROUP
    high = weights.astype(jnp.bfloat16)
    low = (weights - high.astype(jnp.float32)).astype(jnp.bfloat16)
    owner = lax.broadcasted_iota(jnp.int32, (side, count), 0) // GROUP
    expand = (owner == lax.broadcasted_iota(jnp.int32, (side, count), 1)).astype(jnp.float32)
    expand = expand.astype(jnp.bfloat16)
    rows = lax.broadcasted_iota(jnp.int32, (side, side), 0) % GROUP
    same = rows == lax.broadcasted_iota(jnp.int32, (side, side), 1) % GROUP
    for part, out_ref in ((high, high_ref), (low, low_ref)):
        tall = jnp.dot(expand, part, preferred_element_type=jnp.float32).astype(jnp.bfloat16)
        full = lax.dot_general(
            tall, expand, (((1,), (1,)), ((), ())), preferred_element_type=jnp.float32
        )
        out_ref[...] = jnp.where(same, full, 0.0).astype(jnp.bfloat16)


def spread(weights):
    side = weights.shape[0] * GROUP
    shape = jax.ShapeDtypeStruct((side, side), jnp.bfloat16)
    return pl.pallas_call(
        spread_kernel,
        out_shape=[shape, shape],
        compiler_params=pltpu.CompilerParams(vmem_limit_bytes=VMEM),
        name="spread",
    )(weights)


def mix_kernel(high_ref, low_ref, strip_ref, out_ref):
    blocks, pixels, atoms = strip_ref.shape
    flat = strip_ref[...].reshape(blocks * pixels, atoms)
    total = jnp.dot(high_ref[...], flat, preferred_element_type=jnp.float32)
    total += jnp.dot(low_ref[...], flat, preferred_element_type=jnp.float32)
    total = total * total
    out_ref[...] = (total * total).astype(out_ref.dtype).reshape(out_ref.shape)


def mix(high, low, strip):
    blocks, pixels, atoms = strip.shape
    whole = pl.BlockSpec(high.shape, lambda g: (0, 0))
    part = pl.BlockSpec((blocks, GROUP, atoms), lambda g: (0, g, 0))
    return pl.pallas_call(
        mix_kernel,
        out_shape=jax.ShapeDtypeStruct(strip.shape, jnp.bfloat16),
        grid=(pixels // GROUP,),
        in_specs=[whole, whole, part],
        out_specs=part,
        compiler_params=pltpu.CompilerParams(vmem_limit_bytes=VMEM),
        name="mix",
    )(high, low, strip)


def primal_kernel(observed_ref, library_ref, inverse_ref, tile_ref, *rest):
    out_ref = rest[-1]
    library = library_ref[...]
    right = jnp.dot(observed_ref[...], library, preferred_element_type=jnp.float32)
    held = tile_ref[...].astype(jnp.float32)
    if len(rest) > 1:
        held = held + rest[0][...]
    right = right + MU * held
    small = lax.dot_general(
        right.astype(jnp.bfloat16),
        library,
        (((1,), (1,)), ((), ())),
        preferred_element_type=jnp.float32,
    )
    solved = jnp.dot(
        small,
        inverse_ref[...],
        precision=lax.Precision.HIGHEST,
        preferred_element_type=jnp.float32,
    )
    back = jnp.dot(solved.astype(jnp.bfloat16), library, preferred_element_type=jnp.float32)
    primal = (right - back) / MU
    out_ref[...] = primal - rest[0][...] if len(rest) > 1 else primal


def primal_step(observed, library, inverse, tile, dual):
    pixels, atoms = tile.shape
    bands = library.shape[0]
    rows = min(128, pixels)
    wide = pl.BlockSpec((rows, atoms), lambda i: (i, 0))
    specs = [
        pl.BlockSpec((rows, bands), lambda i: (i, 0)),
        pl.BlockSpec((bands, atoms), lambda i: (0, 0)),
        pl.BlockSpec((bands, bands), lambda i: (0, 0)),
        wide,
    ]
    arrays = [observed, library, inverse, tile]
    if dual is not None:
        specs.append(wide)
        arrays.append(dual)
    return pl.pallas_call(
        primal_kernel,
        out_shape=jax.ShapeDtypeStruct((pixels, atoms), jnp.float32),
        grid=(pixels // rows,),
        in_specs=specs,
        out_specs=wide,
        compiler_params=pltpu.CompilerParams(vmem_limit_bytes=VMEM),
        cost_estimate=pl.CostEstimate(
            flops=8 * pixels * atoms * bands, bytes_accessed=12 * pixels * atoms, transcendentals=0
        ),
        name="primal",
    )(*arrays)


def update_kernel(keep_dual, *refs):
    base_ref, averaged_ref, tile_ref, top_ref, bottom_ref, left_ref, right_ref, threshold_ref = (
        refs[:8]
    )
    refs = refs[8:]
    fresh_ref = refs[0]
    new_ref, strip_ref = refs[-2:] if keep_dual else (None, None)
    rows, columns, atoms = tile_ref.shape
    threshold = threshold_ref[...]
    share = 1.0 / (1.0 + GAMMA + ETA)
    left = left_ref[...].astype(jnp.float32)
    right = right_ref[...].astype(jnp.float32)
    place = lax.broadcasted_iota(jnp.int32, (columns, atoms), 0)

    above = top_ref[...].astype(jnp.float32)
    here = tile_ref[0].astype(jnp.float32)
    for row in range(rows):
        below = (tile_ref[row + 1] if row + 1 < rows else bottom_ref[...]).astype(jnp.float32)
        west = jnp.where(place == 0, left[row : row + 1], pltpu.roll(here, 1, 0))
        east = jnp.where(place == columns - 1, right[row : row + 1], pltpu.roll(here, columns - 1, 0))
        spatial = above + below + west + east
        pixels = pl.ds(row * columns, columns)
        base = base_ref[pixels]
        powers = jnp.maximum(averaged_ref[0, pixels].astype(jnp.float32), 1e-36)
        averaged = lax.rsqrt(lax.rsqrt(powers))
        blend = share * base + (share * GAMMA) * averaged + (share * ETA * 0.25) * spatial
        fresh = jnp.maximum(blend - threshold, 0.0)
        rounded = fresh.astype(jnp.bfloat16)
        fresh_ref[pixels] = rounded
        if keep_dual:
            new_ref[pixels] = fresh - base
            strip_ref[0, pixels] = rounded
        above, here = here, below


def update(base, averaged, tile, halo, threshold, keep_dual):
    rows, columns, atoms = tile.shape
    pixels = rows * columns
    width = averaged.shape[2]
    strip = pl.BlockSpec((1, pixels, width), lambda i: (i, 0, 0))
    flat = pl.BlockSpec((pixels, width), lambda i: (0, i))
    specs = [flat, strip, pl.BlockSpec((rows, columns, width), lambda i: (0, 0, i))]
    specs += [pl.BlockSpec((part.shape[0], width), lambda i: (0, i)) for part in halo]
    specs += [pl.BlockSpec((1, width), lambda i: (0, i))]
    arrays = [base, averaged, tile, *halo, threshold.reshape(1, -1)]
    shapes = [jax.ShapeDtypeStruct((pixels, atoms), jnp.bfloat16)]
    if keep_dual:
        shapes.append(jax.ShapeDtypeStruct((pixels, atoms), jnp.float32))
        shapes.append(jax.ShapeDtypeStruct(averaged.shape, jnp.bfloat16))
    return pl.pallas_call(
        functools.partial(update_kernel, keep_dual),
        out_shape=shapes,
        grid=(atoms // width,),
        in_specs=specs,
        out_specs=[flat, flat, strip] if keep_dual else [flat],
        compiler_params=pltpu.CompilerParams(vmem_limit_bytes=VMEM),
        name="update",
    )(*arrays)


def cut(tile, group):
    pixels, atoms = tile.shape
    return tile.reshape(pixels, group, atoms // group).transpose(1, 0, 2)


def local(
    observed, library, warm, match_peer, match_slot, match_count, match_weight, wanted, threshold
):
    tile_rows, tile_cols, atoms = warm.shape
    pixels = tile_rows * tile_cols
    blocks = tile_rows // BLOCK_ROWS
    block_pixels = BLOCK_ROWS * tile_cols
    group = lax.axis_size("col")
    slots = wanted.shape[2]
    coef = coefficients(
        match_peer[:, 0], match_slot[:, 0], match_count[:, 0], match_weight[:, 0], group, slots
    ).astype(jnp.float32)
    hit = wanted[0][:, :, None] == jnp.arange(blocks, dtype=jnp.int32)
    part = jnp.sum(
        jnp.where(hit[None], coef.reshape(blocks, group, slots)[:, :, :, None], 0.0), axis=2
    ).reshape(1, blocks, group * blocks)
    me = lax.axis_index("col")
    got = part
    while got.shape[0] < group:
        ahead = got.shape[0]
        more = got[: group - ahead]
        ring = [(i, (i + ahead) % group) for i in range(group)]
        got = jnp.concatenate([got, lax.ppermute(more, "col", ring)], axis=0)
    steps = jnp.arange(group, dtype=jnp.int32)
    mine = steps[:, None] == lax.rem(me - steps + group, group)[None, :]
    weights = jnp.sum(
        jnp.where(mine[:, :, None, None], got[None], 0.0), axis=1
    ).reshape(group * blocks, group * blocks)
    high, low = spread(weights)

    bands = library.shape[0]
    gram = jnp.dot(library, library.T, preferred_element_type=jnp.float32) + MU * jnp.eye(
        bands, dtype=jnp.float32
    )
    chol = jnp.linalg.cholesky(gram)
    seen = observed.reshape(pixels, -1)
    dual = None
    current = warm
    strips = cut(warm.reshape(pixels, atoms), group)
    for step in range(ITERS):
        strip = lax.all_to_all(strips, "col", split_axis=0, concat_axis=0, tiled=True)
        if step == 0:
            strip, chol = lax.optimization_barrier((strip, chol))
            half = jax.scipy.linalg.solve_triangular(
                chol, jnp.eye(bands, dtype=jnp.float32), lower=True
            )
            inverse = lax.dot_general(
                half, half, (((0,), (0,)), ((), ())), precision=lax.Precision.HIGHEST
            )
        sums = mix(high, low, strip.reshape(group * blocks, block_pixels, -1))
        averaged = lax.all_to_all(
            sums.reshape(strips.shape), "col", split_axis=0, concat_axis=0, tiled=True
        )
        top, bottom = beside(current, "row", 0)
        left, right = beside(current, "col", 1)
        flat = current.reshape(pixels, atoms)
        base = primal_step(seen, library, inverse, flat, dual)
        keep = step + 1 < ITERS
        out = update(
            base, averaged, current, (top, bottom, left, right), threshold, keep
        )
        if keep:
            dual, strips = out[1:]
        current = out[0].reshape(tile_rows, tile_cols, atoms)
    rebuilt = jnp.dot(current.reshape(pixels, atoms), library.T, preferred_element_type=jnp.float32)
    misfit = observed.astype(jnp.float32) - rebuilt.reshape(tile_rows, tile_cols, -1)
    return (current, misfit)


def solution(mesh):
    return jax.shard_map(
        local,
        mesh=mesh,
        in_specs=(
            P("row", "col", None),
            P(),
            P("row", "col", None),
            P("row", "col", None),
            P("row", "col", None),
            P("row", "col"),
            P("row", "col", None),
            P("row", "col", None),
            P(),
        ),
        out_specs=(P("row", "col", None), P("row", "col", None)),
        check_vma=False,
    )
```
